32 devices in a mesh: lat: 4 (over x, core), lon: 8 (over z, y).
Axes of the slice: x: 2, y: 2, z: 4, core: 2. Of those that a mesh axis runs over, the one named last changes fastest.
Arguments:
- grid_latent: bfloat16 [16, 1024, 512], P('lat', 'lon'), may hold values from -6 to 6
- mesh_latent: bfloat16 [4096, 512], P(('lat', 'lon')), may hold values from -6 to 6
- g2m_edges: bfloat16 [65536, 512], P(('lat', 'lon')), may hold values from -6 to 6
- g2m_senders: int32 [32, 2048], P(('lat', 'lon')), may hold values from 0 to 1631, as said below
- g2m_receivers: int32 [32, 2048], P(('lat', 'lon')), may hold values from 0 to 127, as said below
- mm_edges: bfloat16 [65536, 512], P(('lat', 'lon')), may hold values from -6 to 6
- mm_senders: int32 [32, 2048], P(('lat', 'lon')), may hold values from 0 to 639
- mm_receivers: int32 [32, 2048], P(('lat', 'lon')), may hold values from 0 to 128, as said below
- send_rows: int32 [32, 512], P(('lat', 'lon')), may hold values from 0 to 127
- edge_in: bfloat16 [3, 3, 512, 512], replicated, may hold values from -0.15625 to 0.15625
- edge_out: bfloat16 [3, 512, 512], replicated, may hold values from -0.25 to 0.25
- node_in: bfloat16 [3, 2, 512, 512], replicated, may hold values from -0.1875 to 0.1875
- node_out: bfloat16 [3, 512, 512], replicated, may hold values from -0.25 to 0.25
- norm_gain: float32 [3, 2, 512], replicated, may hold values from 0.5 to 1.5
- norm_bias: float32 [3, 2, 512], replicated, may hold values from -1.5 to 1.5
Outputs:
- mesh_out: bfloat16 [4096, 512], P(('lat', 'lon'))
The draws below stay inside these ranges and needn't reach their ends.
Inputs may be any that keep to these rules, and one draw needn't show every extreme that they name: `g2m_receivers`: each patch's edges are sorted by receiver; every mesh node of a patch receives at least one grid-to-mesh edge; the sender cell lies within 4 rows and columns of a cell that is fixed for the receiving node. `g2m_senders`: A flat index into the tile extended by 4 cells, with rows of 136 cells. `mm_receivers`: sorted within a patch; the used slots come first and the unused ones hold 128; some patch uses all 2048 slots in every draw.
All inputs are finite; a program needn't handle non-finite values.
Results may differ from the reference program's by a relative error of at most 0.012.
Values may be sent and summed in bfloat16 or wider, within the bound.
A program may use at most 128 MiB of HBM per device.

```python
import jax
import jax.numpy as jnp
from jax import lax

LATENT = 512
GLAT = 4
GLON = 128
HALO = 4
MESH_DEV = 128
G2M_DEV = 2048
MM_DEV = 2048
CAP = 16
LAYERS = 2
BLOCKS = 3
NLAT = 16
NLON = 1024
MESH = 4096
N_LON = 8
DEVICES = 32


def node_spots(key):
    spot_rows = jax.random.randint(jax.random.fold_in(key, 11), (DEVICES, MESH_DEV), 0, GLAT)
    spot_cols = jax.random.randint(jax.random.fold_in(key, 12), (DEVICES, MESH_DEV), 0, GLON)
    return (spot_rows, spot_cols)


def draw_g2m_receivers(key, part):
    every_node = jnp.broadcast_to(jnp.arange(MESH_DEV, dtype=jnp.int32), (DEVICES, MESH_DEV))
    extra = jax.random.randint(jax.random.fold_in(key, 21), (DEVICES, G2M_DEV - MESH_DEV), 0, MESH_DEV)
    return jnp.sort(jnp.concatenate([every_node, extra.astype(jnp.int32)], axis=1), axis=1).astype(jnp.int32)


def draw_g2m_senders(key, part):
    receivers = draw_g2m_receivers(key, part)
    spot_rows, spot_cols = node_spots(key)
    row_steps = jax.random.randint(jax.random.fold_in(key, 31), (DEVICES, G2M_DEV), 0, 2 * HALO + 1)
    col_steps = jax.random.randint(jax.random.fold_in(key, 32), (DEVICES, G2M_DEV), 0, 2 * HALO + 1)
    cell_rows = jnp.take_along_axis(spot_rows, receivers, axis=1) + row_steps
    cell_cols = jnp.take_along_axis(spot_cols, receivers, axis=1) + col_steps
    return (cell_rows * (GLON + 2 * HALO) + cell_cols).astype(jnp.int32)


def draw_mm_receivers(key, part):
    counts = jax.random.randint(jax.random.fold_in(key, 41), (DEVICES,), MM_DEV // 3, MM_DEV + 1)
    filled = jax.random.randint(jax.random.fold_in(key, 42), (), 0, DEVICES)
    counts = jnp.where(jnp.arange(DEVICES, dtype=jnp.int32) == filled, MM_DEV, counts)
    drawn = jnp.sort(jax.random.randint(jax.random.fold_in(key, 43), (DEVICES, MM_DEV), 0, MESH_DEV), axis=1)
    places = jnp.arange(MM_DEV, dtype=jnp.int32)
    return jnp.where(places[None, :] < counts[:, None], drawn, MESH_DEV).astype(jnp.int32)


def draw_mm_senders(key, part):
    living = draw_mm_receivers(key, part) < MESH_DEV
    branch_pick = jax.random.randint(jax.random.fold_in(key, 51), (DEVICES, MM_DEV), 0, 4)
    faraway = jnp.logical_and(living, branch_pick > 0)
    ranks = jnp.cumsum(faraway.astype(jnp.int32), axis=1) - 1
    slot_total = DEVICES * CAP
    patch_keys = jax.random.split(jax.random.fold_in(key, 53), DEVICES)
    orders = jax.vmap(lambda one_key: jax.random.permutation(one_key, slot_total))(patch_keys).astype(jnp.int32)
    positions = (jnp.maximum(ranks, 0) % slot_total).astype(jnp.int32)
    remote = MESH_DEV + jnp.take_along_axis(orders, positions, axis=1)
    nearby = jax.random.randint(jax.random.fold_in(key, 52), (DEVICES, MM_DEV), 0, MESH_DEV)
    return jnp.where(faraway, remote, nearby).astype(jnp.int32)


def plant(values, own_key, least, high):
    longest = values.shape.index(max(values.shape))
    spots = []
    for shift in (0, 1):
        where = [jax.random.randint(jax.random.fold_in(own_key, axis), (), 0, length) for axis, length in enumerate(values.shape)]
        where[longest] = (where[longest] + shift) % values.shape[longest]
        spots.append(tuple(where))
    return values.at[spots[0]].set(least).at[spots[1]].set(high)


def block_levels(own_key, dims, cuts, low, top_value):
    level, own = 1.0, jax.random.fold_in(own_key, 6)
    for axis_at, parts in cuts:
        heights = jnp.exp(jax.random.uniform(jax.random.fold_in(own, axis_at), (parts,), jnp.float32, low / len(cuts), top_value / len(cuts)))
        level = level * jnp.repeat(heights, dims[axis_at] // parts).reshape([-1 if axis == axis_at else 1 for axis in range(len(dims))])
    return level


def scatter_about(stream_key, dims, scale, limit, pieces=(), kind=jnp.bfloat16):
    values = jax.random.normal(stream_key, dims, jnp.float32) * scale
    if len(pieces) > 0:
        values = block_levels(stream_key, dims, pieces, -0.22, 0.18) * values
    return jnp.clip(values, min=-limit, max=limit).astype(kind)


def setup_inputs(seed: int = 0) -> dict:
    key_of = jax.random.split(jax.random.key(seed), 16)
    return {
        "grid_latent": scatter_about(key_of[0], (NLAT, NLON, LATENT), 1.0, 6.0, ((0, 4), (1, 8))),
        "mesh_latent": scatter_about(key_of[1], (MESH, LATENT), 1.0, 6.0, ((0, 32),)),
        "g2m_edges": scatter_about(key_of[2], (DEVICES * G2M_DEV, LATENT), 1.0, 6.0, ((0, 32),)),
        "g2m_senders": draw_g2m_senders(jax.random.fold_in(key_of[15], 71), 0),
        "g2m_receivers": draw_g2m_receivers(jax.random.fold_in(key_of[15], 71), 0),
        "mm_edges": scatter_about(key_of[5], (DEVICES * MM_DEV, LATENT), 1.0, 6.0, ((0, 32),)),
        "mm_senders": draw_mm_senders(jax.random.fold_in(key_of[15], 71), 0),
        "mm_receivers": draw_mm_receivers(jax.random.fold_in(key_of[15], 71), 0),
        "send_rows": plant(jax.random.randint(key_of[8], (DEVICES, DEVICES * CAP), 0, MESH_DEV), jax.random.fold_in(key_of[8], 1), 0, MESH_DEV - 1).astype(jnp.int32),
        "edge_in": scatter_about(key_of[9], (BLOCKS, 3, LATENT, LATENT), (3 * LATENT) ** -0.5, 0.15625),
        "edge_out": scatter_about(key_of[10], (BLOCKS, LATENT, LATENT), LATENT ** -0.5, 0.25),
        "node_in": scatter_about(key_of[11], (BLOCKS, 2, LATENT, LATENT), (2 * LATENT) ** -0.5, 0.1875),
        "node_out": scatter_about(key_of[12], (BLOCKS, LATENT, LATENT), LATENT ** -0.5, 0.25),
        "norm_gain": jnp.clip(1.0 + 0.1 * jax.random.normal(key_of[13], (BLOCKS, 2, LATENT), jnp.float32), 0.5, 1.5),
        "norm_bias": scatter_about(key_of[14], (BLOCKS, 2, LATENT), 0.3, 1.5, (), jnp.float32),
    }


NORM_EPS = 1e-05

def normalize(values, gains, biases):
    centre = lax.optimization_barrier(jnp.mean(values, axis=-1, keepdims=True))
    spread = lax.optimization_barrier(jnp.mean(jnp.square(values - centre), axis=-1, keepdims=True))
    return (values - centre) * lax.rsqrt(spread + NORM_EPS) * gains + biases

def project(values, weights):
    return jnp.dot(values, weights, preferred_element_type=jnp.float32).astype(jnp.bfloat16)

def edge_update(edge_rows, sender_terms, receiver_terms, weights_in, weights_out, gains, biases):
    pre_act = jnp.dot(edge_rows, weights_in, preferred_element_type=jnp.float32)
    pre_act = pre_act + sender_terms.astype(jnp.float32) + receiver_terms.astype(jnp.float32)
    hidden = jax.nn.silu(pre_act).astype(jnp.bfloat16)
    output = jnp.dot(hidden, weights_out, preferred_element_type=jnp.float32)
    return (edge_rows.astype(jnp.float32) + normalize(output, gains, biases)).astype(jnp.bfloat16)

def node_update(nodes, summed, weights_in, weights_out, gains, biases):
    pre_act = jnp.dot(nodes, weights_in[0], preferred_element_type=jnp.float32)
    pre_act = pre_act + jnp.dot(summed.astype(jnp.bfloat16), weights_in[1], preferred_element_type=jnp.float32)
    hidden = jax.nn.silu(pre_act).astype(jnp.bfloat16)
    output = jnp.dot(hidden, weights_out, preferred_element_type=jnp.float32)
    return (nodes.astype(jnp.float32) + normalize(output, gains, biases)).astype(jnp.bfloat16)

def reference(grid_latent, mesh_latent, g2m_edges, g2m_senders, g2m_receivers, mm_edges, mm_senders, mm_receivers, send_rows, edge_in, edge_out, node_in, node_out, norm_gain, norm_bias):
    device_ids = jnp.arange(DEVICES, dtype=jnp.int32)
    grid_terms = project(grid_latent.reshape(-1, LATENT), edge_in[0, 1]).reshape(NLAT, NLON, LATENT)
    wrapped = jnp.concatenate([grid_terms[:, NLON - HALO:], grid_terms, grid_terms[:, :HALO]], axis=1)
    padded = jnp.pad(wrapped, ((HALO, HALO), (0, 0), (0, 0)))
    lookup = padded.reshape(-1, LATENT)
    tile_width = GLON + 2 * HALO
    lat_ids = device_ids // N_LON
    lon_ids = device_ids % N_LON
    glob_rows = lat_ids[:, None] * GLAT + g2m_senders // tile_width
    glob_cols = lon_ids[:, None] * GLON + g2m_senders % tile_width
    glob_send = (glob_rows * (NLON + 2 * HALO) + glob_cols).astype(jnp.int32)
    receiver_table = project(mesh_latent, edge_in[0, 2])

    def encode_device(items):
        edge_rows, senders, receivers, device = items
        sent = jnp.take(lookup, senders, axis=0)
        got = jnp.take(receiver_table, device * MESH_DEV + receivers, axis=0)
        updated = edge_update(edge_rows, sent, got, edge_in[0, 0], edge_out[0], norm_gain[0, 0], norm_bias[0, 0])
        return jax.ops.segment_sum(updated.astype(jnp.float32), receivers, num_segments=MESH_DEV)
    summed = lax.map(encode_device, (g2m_edges.reshape(DEVICES, G2M_DEV, LATENT), glob_send, g2m_receivers, device_ids))
    mesh_nodes = node_update(mesh_latent, summed.reshape(-1, LATENT), node_in[0], node_out[0], norm_gain[0, 1], norm_bias[0, 1])
    sources = send_rows.reshape(DEVICES, DEVICES, CAP) + (device_ids * MESH_DEV)[:, None, None]
    remote_index = jnp.transpose(sources, (1, 0, 2)).reshape(DEVICES, DEVICES * CAP).astype(jnp.int32)
    nearby = mm_senders < MESH_DEV
    far_index = jnp.take_along_axis(remote_index, jnp.clip(mm_senders - MESH_DEV, 0, DEVICES * CAP - 1).astype(jnp.int32), axis=1)
    glob_mm = jnp.where(nearby, device_ids[:, None] * MESH_DEV + mm_senders, far_index).astype(jnp.int32)
    alive = mm_receivers < MESH_DEV
    local_recv = jnp.minimum(mm_receivers, MESH_DEV - 1).astype(jnp.int32)
    edge_state = mm_edges.reshape(DEVICES, MM_DEV, LATENT)
    for level in range(1, LAYERS + 1):
        sender_table = project(mesh_nodes, edge_in[level, 1])
        recv_table = project(mesh_nodes, edge_in[level, 2])

        def process_device(items):
            edge_rows, senders, receivers, living, device = items
            sent = jnp.take(sender_table, senders, axis=0)
            got = jnp.take(recv_table, device * MESH_DEV + receivers, axis=0)
            updated = edge_update(edge_rows, sent, got, edge_in[level, 0], edge_out[level], norm_gain[level, 0], norm_bias[level, 0])
            kept = jnp.where(living[:, None], updated.astype(jnp.float32), jnp.float32(0.0))
            return (updated, jax.ops.segment_sum(kept, receivers, num_segments=MESH_DEV))
        edge_state, summed = lax.map(process_device, (edge_state, glob_mm, local_recv, alive, device_ids))
        mesh_nodes = node_update(mesh_nodes, summed.reshape(-1, LATENT), node_in[level], node_out[level], norm_gain[level, 1], norm_bias[level, 1])
    return mesh_nodes
```

```python
import functools

import jax
import jax.numpy as jnp
from jax import lax
from jax.experimental import pallas as pl
from jax.experimental.pallas import tpu as pltpu
from jax.sharding import PartitionSpec as P

HALO = 4
NORM_EPS = 1e-05
LANES = 128
ROWS = 256
GROUP = 2
MESH_IDS = pl.DeviceIdType.MESH
BF16 = jnp.bfloat16
F32 = jnp.float32


def dot(a, b):
    return jnp.dot(a, b, preferred_element_type=F32)


def silu(v):
    half = 0.5 * v
    return half + half * jnp.tanh(half)


def layer_norm(values, gain, bias):
    scale = 1.0 / values.shape[-1]
    centre = jnp.sum(values, axis=-1, keepdims=True) * scale
    away = values - centre
    spread = jnp.sum(away * away, axis=-1, keepdims=True) * scale
    return away * lax.rsqrt(spread + NORM_EPS) * gain + bias


def onehot(idx, base, width):
    lane = lax.broadcasted_iota(jnp.int32, idx.shape, 1)
    parts = [
        jnp.where(idx == lane + (base + j), 1.0, 0.0).astype(BF16)
        for j in range(0, width, LANES)
    ]
    return parts[0] if len(parts) == 1 else jnp.concatenate(parts, axis=1)


def kernel(
    n_lat, n_lon, tile_rows, tile_cols, blocks,
    grid_hbm, mesh_ref, g2m_hbm, g2m_s_ref, g2m_r_ref, mm_hbm, mm_s_ref, mm_r_ref, send_ref,
    ein_hbm, eout_hbm, nin_hbm, nout_hbm, gain_ref, bias_ref,
    out_ref,
    grid_v, edge_v, mme_v, pre, tab, stk, wproj, eout, nin, nout,
    packs, picks, sel_send, idx_a, idx_b, idx_c, idx_d, nodes,
    w_sem, halo_send, halo_recv, a2a_send, a2a_recv,
):
    lat, lon = lax.axis_index("lat"), lax.axis_index("lon")
    n_dev = n_lat * n_lon
    me = lat * n_lon + lon
    width = mesh_ref.shape[1]
    node_count = mesh_ref.shape[0]
    cells = tile_rows * tile_cols
    cap = send_ref.shape[1] // n_dev
    barrier = pltpu.get_barrier_semaphore()

    def place(d):
        return (d // n_lon, d % n_lon)

    def greet(off, carry):
        d = (me + off) % n_dev
        pl.semaphore_signal(barrier, inc=1, device_id=place(d), device_id_type=MESH_IDS)
        return carry

    lax.fori_loop(1, n_dev, greet, 0)

    def load(src, dst, at):
        copy = pltpu.make_async_copy(src, dst, w_sem.at[at])
        copy.start()
        return copy

    own_at, north_at, south_at = width, width + cells, width + 2 * cells
    side_at = width + 3 * cells
    recv_at = side_at + LANES

    c_grid = load(grid_hbm, grid_v, 0)
    c_proj0 = load(ein_hbm.at[0, 1], wproj.at[0, 0], 1)
    c_w0 = load(ein_hbm.at[0, 0], tab.at[pl.ds(0, width)], 2)
    c_g2m = load(g2m_hbm, edge_v, 3)
    c_recv0 = load(ein_hbm.at[0, 2], wproj.at[0, 1], 4)

    tall = tile_rows + 2 * HALO
    wide = tile_cols + 2 * HALO
    zero_rows = functools.partial(jnp.zeros, dtype=BF16)
    side_rows = 2 * tall * HALO
    tab[side_at + side_rows:recv_at, :] = zero_rows((LANES - side_rows, width))
    block = tile_rows * HALO

    @pl.when(lat == 0)
    def _():
        tab[north_at:north_at + cells, :] = zero_rows((cells, width))
        tab[side_at:side_at + block, :] = zero_rows((block, width))
        tab[side_at + 3 * block:side_at + 4 * block, :] = zero_rows((block, width))

    @pl.when(lat == n_lat - 1)
    def _():
        tab[south_at:south_at + cells, :] = zero_rows((cells, width))
        tab[side_at + 2 * block:side_at + 3 * block, :] = zero_rows((block, width))
        tab[side_at + 5 * block:side_at + 6 * block, :] = zero_rows((block, width))

    c_grid.wait()
    c_proj0.wait()
    firsts, lasts = [], []
    for r in range(tile_rows):
        term = dot(grid_v[r], wproj[0, 0])
        tab[own_at + r * tile_cols:own_at + (r + 1) * tile_cols, :] = term.astype(BF16)
        firsts.append(term[:HALO])
        lasts.append(term[tile_cols - HALO:])
    packs[0:block, :] = jnp.concatenate(firsts, axis=0).astype(BF16)
    packs[block:2 * block, :] = jnp.concatenate(lasts, axis=0).astype(BF16)

    pl.semaphore_wait(barrier, n_dev - 1)

    own = tab.at[pl.ds(own_at, cells)]
    east, west = (lon + 1) % n_lon, (lon + n_lon - 1) % n_lon

    def halo(at, src, dst_row, count, to):
        return pltpu.make_async_remote_copy(
            src_ref=src, dst_ref=tab.at[pl.ds(dst_row, count)],
            send_sem=halo_send.at[at], recv_sem=halo_recv.at[at],
            device_id=to, device_id_type=MESH_IDS,
        )

    first_cols, last_cols = packs.at[pl.ds(0, block)], packs.at[pl.ds(block, block)]
    to_north = [
        halo(0, own, south_at, cells, (lat - 1, lon)),
        halo(1, last_cols, side_at + 2 * block, block, (lat - 1, east)),
        halo(2, first_cols, side_at + 5 * block, block, (lat - 1, west)),
    ]
    to_south = [
        halo(3, own, north_at, cells, (lat + 1, lon)),
        halo(4, last_cols, side_at, block, (lat + 1, east)),
        halo(5, first_cols, side_at + 3 * block, block, (lat + 1, west)),
    ]
    to_level = [
        halo(6, last_cols, side_at + block, block, (lat, east)),
        halo(7, first_cols, side_at + 4 * block, block, (lat, west)),
    ]

    @pl.when(lat > 0)
    def _():
        for c in to_north:
            c.start()

    @pl.when(lat < n_lat - 1)
    def _():
        for c in to_south:
            c.start()

    for c in to_level:
        c.start()

    c_eout, c_nin, c_nout, c_w, c_ps, c_pr = [], [], [], [None], [None], [None]
    at = 5
    for k in range(blocks):
        if k == 1:
            c_mm = load(mm_hbm, mme_v, at)
            at += 1
        if k > 0:
            c_ps.append(load(ein_hbm.at[k, 1], wproj.at[k, 0], at))
            c_pr.append(load(ein_hbm.at[k, 2], wproj.at[k, 1], at + 1))
            c_w.append(load(ein_hbm.at[k, 0], stk.at[k - 1, pl.ds(0, width)], at + 2))
            at += 3
        c_eout.append(load(eout_hbm.at[k], eout.at[k], at))
        c_nin.append(load(nin_hbm.at[k], nin.at[k], at + 1))
        c_nout.append(load(nout_hbm.at[k], nout.at[k], at + 2))
        at += 3

    senders = g2m_s_ref[...]
    row = jnp.zeros_like(senders)
    for r in range(1, tall):
        row = row + jnp.where(senders >= r * wide, 1, 0)
    col = senders - row * wide
    west_spot = 3 * cells + row * HALO + col
    east_spot = 3 * cells + (tall + row) * HALO + (col - (wide - HALO))
    spot = jnp.where(
        col < HALO, west_spot,
        jnp.where(col >= wide - HALO, east_spot, row * tile_cols + col - HALO),
    )

    def spread_rows(values, dst):
        for j in range(0, values.shape[1], LANES):
            piece = jnp.broadcast_to(values[:, j:j + LANES], (LANES, LANES))
            dst[j:j + LANES, :] = piece.T

    spread_rows(spot, idx_a)
    spread_rows(g2m_r_ref[...], idx_b)
    spread_rows(mm_s_ref[...], idx_c)
    spread_rows(jnp.minimum(mm_r_ref[...], node_count - 1), idx_d)
    sends = send_ref[...]
    for j in range(0, sends.shape[1], LANES):
        piece = jnp.broadcast_to(sends[:, j:j + LANES], (LANES, LANES)).T
        sel_send[j:j + LANES, :] = onehot(piece, 0, node_count)

    def over_rows(count, body):
        def step(i, carry):
            for g in range(GROUP):
                body(pl.ds(pl.multiple_of((i * GROUP + g) * ROWS, ROWS), ROWS))
            return carry

        lax.fori_loop(0, count // (ROWS * GROUP), step, 0)

    def finish_edges(rows, acc, edges, k):
        hidden = silu(acc).astype(BF16)
        normed = layer_norm(dot(hidden, eout[k]), gain_ref[k, 0:1, :], bias_ref[k, 0:1, :])
        edges[rows, :] = (edges[rows, :].astype(F32) + normed).astype(BF16)

    def gather_sum(recv_ref, edges):
        node = lax.broadcasted_iota(jnp.int32, (node_count, recv_ref.shape[1]), 0)
        incidence = jnp.where(node == recv_ref[...], 1.0, 0.0).astype(BF16)
        return dot(incidence, edges[...])

    def node_step(current, summed, k):
        c_nin[k].wait()
        c_nout[k].wait()
        joined = jnp.concatenate([current, summed.astype(BF16)], axis=1)
        hidden = silu(dot(joined, nin[k])).astype(BF16)
        normed = layer_norm(dot(hidden, nout[k]), gain_ref[k, 1:2, :], bias_ref[k, 1:2, :])
        return (current.astype(F32) + normed).astype(BF16)

    c_w0.wait()
    c_g2m.wait()

    def enc_first(rows):
        joined = jnp.concatenate([edge_v[rows, :], onehot(idx_a[rows, :], cells, cells)], axis=1)
        pre[rows, :] = dot(joined, tab[0:width + cells, :])

    over_rows(edge_v.shape[0], enc_first)
    c_recv0.wait()
    tab[recv_at:recv_at + node_count, :] = dot(mesh_ref[...], wproj[0, 1]).astype(BF16)
    c_eout[0].wait()

    for c in to_level:
        c.wait()

    @pl.when(lat > 0)
    def _():
        for c in to_north:
            c.wait_send()
        for c in to_south:
            c.wait_recv()

    @pl.when(lat < n_lat - 1)
    def _():
        for c in to_south:
            c.wait_send()
        for c in to_north:
            c.wait_recv()

    def enc_second(rows):
        spots = idx_a[rows, :]
        joined = jnp.concatenate(
            [
                onehot(spots, 0, cells),
                onehot(spots, 2 * cells, cells + LANES),
                onehot(idx_b[rows, :], 0, node_count),
            ],
            axis=1,
        )
        acc = pre[rows, :] + dot(joined, tab[north_at:recv_at + node_count, :])
        finish_edges(rows, acc, edge_v, 0)

    over_rows(edge_v.shape[0], enc_second)
    nodes[...] = node_step(mesh_ref[...], gather_sum(g2m_r_ref, edge_v), 0)

    r_at, s_at, arr_at = width, width + node_count, width + 2 * node_count
    for k in range(1, blocks):
        table, pick = stk.at[k - 1], picks.at[k - 1]
        current = nodes[...]
        c_ps[k].wait()
        outgoing = dot(current, wproj[k, 0]).astype(BF16)
        pick[...] = dot(sel_send[...], outgoing).astype(BF16)

        def exchange(d, src_at, sem_at, to):
            return pltpu.make_async_remote_copy(
                src_ref=pick.at[pl.ds(pl.multiple_of(d * cap, cap), cap)],
                dst_ref=table.at[pl.ds(pl.multiple_of(arr_at + src_at * cap, cap), cap)],
                send_sem=a2a_send.at[k - 1, d], recv_sem=a2a_recv.at[k - 1, sem_at],
                device_id=place(to), device_id_type=MESH_IDS,
            )

        def send(off, carry):
            d = (me + off) % n_dev
            exchange(d, me, me, d).start()
            return carry

        lax.fori_loop(1, n_dev, send, 0)
        table[pl.ds(pl.multiple_of(arr_at + me * cap, cap), cap), :] = pick[
            pl.ds(pl.multiple_of(me * cap, cap), cap), :
        ]
        table[s_at:s_at + node_count, :] = outgoing
        c_pr[k].wait()
        table[r_at:r_at + node_count, :] = dot(current, wproj[k, 1]).astype(BF16)
        c_w[k].wait()
        if k == 1:
            c_mm.wait()

        def mm_first(rows):
            joined = jnp.concatenate(
                [
                    mme_v[rows, :],
                    onehot(idx_d[rows, :], 0, node_count),
                    onehot(idx_c[rows, :], 0, node_count),
                ],
                axis=1,
            )
            pre[rows, :] = dot(joined, table[0:arr_at, :])

        over_rows(mme_v.shape[0], mm_first)
        c_eout[k].wait()

        def arrive(off, carry):
            d = (me + off) % n_dev
            exchange(d, d, d, d).wait()
            return carry

        lax.fori_loop(1, n_dev, arrive, 0)

        def mm_second(rows):
            picked = onehot(idx_c[rows, :], node_count, n_dev * cap)
            acc = pre[rows, :] + dot(picked, table[arr_at:arr_at + n_dev * cap, :])
            finish_edges(rows, acc, mme_v, k)

        over_rows(mme_v.shape[0], mm_second)
        updated = node_step(current, gather_sum(mm_r_ref, mme_v), k)
        if k < blocks - 1:
            nodes[...] = updated
        else:
            out_ref[...] = updated


def local(
    n_lat, n_lon,
    grid_latent, mesh_latent, g2m_edges, g2m_senders, g2m_receivers, mm_edges, mm_senders,
    mm_receivers, send_rows, edge_in, edge_out, node_in, node_out, norm_gain, norm_bias,
):
    tile_rows, tile_cols, width = grid_latent.shape
    blocks = edge_in.shape[0]
    node_count = mesh_latent.shape[0]
    n_dev = n_lat * n_lon
    edges, mm = g2m_edges.shape[0], mm_edges.shape[0]
    sends = send_rows.shape[1]
    assert tile_rows == HALO and node_count == LANES and tile_cols % LANES == 0
    node_in = node_in.reshape(blocks, 2 * width, width)
    hbm, vmem = pl.BlockSpec(memory_space=pl.ANY), pl.BlockSpec(memory_space=pltpu.VMEM)
    table_rows = width + 3 * tile_rows * tile_cols + LANES + node_count
    dma = pltpu.SemaphoreType.DMA
    return pl.pallas_call(
        functools.partial(kernel, n_lat, n_lon, tile_rows, tile_cols, blocks),
        out_shape=jax.ShapeDtypeStruct((node_count, width), BF16),
        in_specs=[hbm, vmem, hbm, vmem, vmem, hbm, vmem, vmem, vmem, hbm, hbm, hbm, hbm, vmem, vmem],
        out_specs=vmem,
        scratch_shapes=[
            pltpu.VMEM((tile_rows, tile_cols, width), BF16),
            pltpu.VMEM((edges, width), BF16),
            pltpu.VMEM((mm, width), BF16),
            pltpu.VMEM((max(edges, mm), width), F32),
            pltpu.VMEM((table_rows, width), BF16),
            pltpu.VMEM((blocks - 1, width + 2 * node_count + sends, width), BF16),
            pltpu.VMEM((blocks, 2, width, width), BF16),
            pltpu.VMEM((blocks, width, width), BF16),
            pltpu.VMEM((blocks, 2 * width, width), BF16),
            pltpu.VMEM((blocks, width, width), BF16),
            pltpu.VMEM((2 * tile_rows * HALO, width), BF16),
            pltpu.VMEM((blocks - 1, sends, width), BF16),
            pltpu.VMEM((sends, node_count), BF16),
            pltpu.VMEM((edges, LANES), jnp.int32),
            pltpu.VMEM((edges, LANES), jnp.int32),
            pltpu.VMEM((mm, LANES), jnp.int32),
            pltpu.VMEM((mm, LANES), jnp.int32),
            pltpu.VMEM((node_count, width), BF16),
            dma((6 + 6 * blocks,)),
            dma((8,)),
            dma((8,)),
            dma((blocks - 1, n_dev)),
            dma((blocks - 1, n_dev)),
        ],
        compiler_params=pltpu.CompilerParams(
            collective_id=0, has_side_effects=True, vmem_limit_bytes=56 * 1024 * 1024
        ),
        name="encode_process",
    )(
        grid_latent, mesh_latent, g2m_edges, g2m_senders, g2m_receivers, mm_edges, mm_senders,
        mm_receivers, send_rows, edge_in, edge_out, node_in, node_out, norm_gain, norm_bias,
    )


def solution(mesh):
    tiles = P(("lat", "lon"), None)
    in_specs = (P("lat", "lon", None),) + (tiles,) * 8 + (P(),) * 6
    body = functools.partial(local, mesh.shape["lat"], mesh.shape["lon"])
    return jax.shard_map(body, mesh=mesh, in_specs=in_specs, out_specs=tiles, check_vma=False)
```

```python
import functools
import math

import jax
import jax.numpy as jnp
from jax import lax
from jax.experimental import pallas as pl
from jax.experimental.pallas import tpu as pltpu
from jax.sharding import PartitionSpec as P

HALO = 4
NORM_EPS = 1e-05
LANES = 128
ROWS = 256
GROUP = 4
MESH_IDS = pl.DeviceIdType.MESH
BF16 = jnp.bfloat16
F32 = jnp.float32


def dot(a, b):
    return jnp.dot(a, b, preferred_element_type=F32)


def silu(v):
    half = 0.5 * v
    return half + half * jnp.tanh(half)


def layer_norm(values, gain, bias):
    scale = 1.0 / values.shape[-1]
    centre = jnp.sum(values, axis=-1, keepdims=True) * scale
    away = values - centre
    spread = jnp.sum(away * away, axis=-1, keepdims=True) * scale
    return away * lax.rsqrt(spread + NORM_EPS) * gain + bias


def onehot(idx, base, width):
    lane = lax.broadcasted_iota(jnp.int32, idx.shape, 1)
    parts = [
        jnp.where(idx == lane + (base + j), 1.0, 0.0).astype(BF16)
        for j in range(0, width, LANES)
    ]
    return parts[0] if len(parts) == 1 else jnp.concatenate(parts, axis=1)


def kernel(
    n_lat, n_lon, tile_rows, tile_cols, blocks,
    grid_hbm, mesh_hbm, g2m_hbm, g2m_s_hbm, g2m_r_hbm, mm_hbm, mm_s_hbm, mm_r_hbm, send_hbm,
    ein_hbm, eout_hbm, nin_hbm, nout_hbm, gain_hbm, bias_hbm,
    out_ref,
    mesh_ref, g2m_s_ref, g2m_r_ref, mm_s_ref, mm_r_ref, send_ref, gain_ref, bias_ref,
    sel_arr, inc_g, inc_m, sums, grid_v, edge_v, mme_v, pre, tab, stk, wproj, eout, nin, nout,
    packs, picks, sel_send, idx_a, idx_b, idx_c, idx_d, nodes,
    w_sem, halo_send, halo_recv, a2a_send, a2a_recv,
):
    lat, lon = lax.axis_index("lat"), lax.axis_index("lon")
    n_dev = n_lat * n_lon
    me = lat * n_lon + lon
    width = mesh_ref.shape[1]
    node_count = mesh_ref.shape[0]
    cells = tile_rows * tile_cols
    cap = send_ref.shape[1] // n_dev
    barrier = pltpu.get_barrier_semaphore()

    def place(d):
        return (d // n_lon, d % n_lon)

    def greet(off, carry):
        d = (me + off) % n_dev
        pl.semaphore_signal(barrier, inc=1, device_id=place(d), device_id_type=MESH_IDS)
        return carry


    def load(src, dst, at):
        copy = pltpu.make_async_copy(src, dst, w_sem.at[at])
        copy.start()
        return copy

    own_at, north_at, south_at = width, width + cells, width + 2 * cells
    side_at = width + 3 * cells
    recv_at = side_at + LANES

    c_grid = load(grid_hbm, grid_v, 0)
    c_proj0 = load(ein_hbm.at[0, 1], wproj.at[0, 0], 1)
    c_w0 = load(ein_hbm.at[0, 0], tab.at[pl.ds(0, width)], 2)
    c_g2m = load(g2m_hbm, edge_v, 3)
    c_recv0 = load(ein_hbm.at[0, 2], wproj.at[0, 1], 4)
    small = [
        load(src, dst, 5 + i)
        for i, (src, dst) in enumerate((
            (g2m_s_hbm, g2m_s_ref), (g2m_r_hbm, g2m_r_ref), (mm_s_hbm, mm_s_ref),
            (mm_r_hbm, mm_r_ref), (send_hbm, send_ref), (mesh_hbm, mesh_ref),
            (gain_hbm, gain_ref), (bias_hbm, bias_ref),
        ))
    ]
    lax.fori_loop(1, n_dev, greet, 0)

    tall = tile_rows + 2 * HALO
    wide = tile_cols + 2 * HALO
    zero_rows = functools.partial(jnp.zeros, dtype=BF16)
    side_rows = 2 * tall * HALO
    tab[side_at + side_rows:recv_at, :] = zero_rows((LANES - side_rows, width))
    block = tile_rows * HALO

    @pl.when(lat == 0)
    def _():
        tab[north_at:north_at + cells, :] = zero_rows((cells, width))
        tab[side_at:side_at + block, :] = zero_rows((block, width))
        tab[side_at + 3 * block:side_at + 4 * block, :] = zero_rows((block, width))

    @pl.when(lat == n_lat - 1)
    def _():
        tab[south_at:south_at + cells, :] = zero_rows((cells, width))
        tab[side_at + 2 * block:side_at + 3 * block, :] = zero_rows((block, width))
        tab[side_at + 5 * block:side_at + 6 * block, :] = zero_rows((block, width))

    c_grid.wait()
    c_proj0.wait()
    firsts, lasts = [], []
    for r in range(tile_rows):
        term = dot(grid_v[r], wproj[0, 0])
        tab[own_at + r * tile_cols:own_at + (r + 1) * tile_cols, :] = term.astype(BF16)
        firsts.append(term[:HALO])
        lasts.append(term[tile_cols - HALO:])
    packs[0:block, :] = jnp.concatenate(firsts, axis=0).astype(BF16)
    packs[block:2 * block, :] = jnp.concatenate(lasts, axis=0).astype(BF16)

    pl.semaphore_wait(barrier, n_dev - 1)

    own = tab.at[pl.ds(own_at, cells)]
    east, west = (lon + 1) % n_lon, (lon + n_lon - 1) % n_lon

    def halo(at, src, dst_row, count, to):
        return pltpu.make_async_remote_copy(
            src_ref=src, dst_ref=tab.at[pl.ds(dst_row, count)],
            send_sem=halo_send.at[at], recv_sem=halo_recv.at[at],
            device_id=to, device_id_type=MESH_IDS,
        )

    first_cols, last_cols = packs.at[pl.ds(0, block)], packs.at[pl.ds(block, block)]
    to_north = [
        halo(0, own, south_at, cells, (lat - 1, lon)),
        halo(1, last_cols, side_at + 2 * block, block, (lat - 1, east)),
        halo(2, first_cols, side_at + 5 * block, block, (lat - 1, west)),
    ]
    to_south = [
        halo(3, own, north_at, cells, (lat + 1, lon)),
        halo(4, last_cols, side_at, block, (lat + 1, east)),
        halo(5, first_cols, side_at + 3 * block, block, (lat + 1, west)),
    ]
    to_level = [
        halo(6, last_cols, side_at + block, block, (lat, east)),
        halo(7, first_cols, side_at + 4 * block, block, (lat, west)),
    ]

    for c in to_level:
        c.start()

    @pl.when(lat > 0)
    def _():
        for c in reversed(to_north):
            c.start()

    @pl.when(lat < n_lat - 1)
    def _():
        for c in reversed(to_south):
            c.start()

    c_eout, c_nin, c_nout, c_w, c_ps, c_pr = [], [], [], [None], [None], [None]
    at = 5 + len(small)
    for k in range(blocks):
        if k == 1:
            c_mm = load(mm_hbm, mme_v, at)
            at += 1
        if k > 0:
            c_ps.append(load(ein_hbm.at[k, 1], wproj.at[k, 0], at))
            c_pr.append(load(ein_hbm.at[k, 2], wproj.at[k, 1], at + 1))
            c_w.append(load(ein_hbm.at[k, 0], stk.at[k - 1, pl.ds(0, width)], at + 2))
            at += 3
        c_eout.append(load(eout_hbm.at[k], eout.at[k], at))
        c_nin.append(load(nin_hbm.at[k], nin.at[k], at + 1))
        c_nout.append(load(nout_hbm.at[k], nout.at[k], at + 2))
        at += 3

    for c in small:
        c.wait()

    senders = g2m_s_ref[...]
    row = jnp.zeros_like(senders)
    for r in range(1, tall):
        row = row + jnp.where(senders >= r * wide, 1, 0)
    col = senders - row * wide
    west_spot = 3 * cells + row * HALO + col
    east_spot = 3 * cells + (tall + row) * HALO + (col - (wide - HALO))
    spot = jnp.where(
        col < HALO, west_spot,
        jnp.where(col >= wide - HALO, east_spot, row * tile_cols + col - HALO),
    )

    def spread_rows(values, dst):
        for j in range(0, values.shape[1], LANES):
            piece = jnp.broadcast_to(values[:, j:j + LANES], (LANES, LANES))
            dst[j:j + LANES, :] = piece.T

    spread_rows(spot, idx_a)
    spread_rows(g2m_r_ref[...], idx_b)
    spread_rows(mm_s_ref[...], idx_c)
    spread_rows(jnp.minimum(mm_r_ref[...], node_count - 1), idx_d)
    sends = send_ref[...]
    for j in range(0, sends.shape[1], LANES):
        piece = jnp.broadcast_to(sends[:, j:j + LANES], (LANES, LANES)).T
        sel_send[j:j + LANES, :] = onehot(piece, 0, node_count)

    def over_rows(count, body):
        def step(i, carry):
            for g in range(GROUP):
                body(pl.ds(pl.multiple_of((i * GROUP + g) * ROWS, ROWS), ROWS))
            return carry

        lax.fori_loop(0, count // (ROWS * GROUP), step, 0)

    def mark_receivers(recv_ref, dst):
        node = lax.broadcasted_iota(jnp.int32, dst.shape, 0)
        dst[...] = jnp.where(node == recv_ref[...], 1.0, 0.0).astype(BF16)

    def finish_edges(first, edges, incidence, k):
        sums[...] = jnp.zeros_like(sums)
        gain, bias = gain_ref[k, 0:1, :], bias_ref[k, 0:1, :]

        def step(i, carry):
            spans = [
                pl.ds(pl.multiple_of((i * GROUP + g) * ROWS, ROWS), ROWS) for g in range(GROUP)
            ]
            total = sums[...]
            done = []
            ahead = first(spans[0])
            for g, rows in enumerate(spans):
                acc = ahead
                if g + 1 < GROUP:
                    ahead = first(spans[g + 1])
                hidden = silu(acc).astype(BF16)
                normed = layer_norm(dot(hidden, eout[k]), gain, bias)
                new = (edges[rows, :].astype(F32) + normed).astype(BF16)
                total = total + dot(incidence[:, rows], new)
                done.append(new)
            for rows, new in zip(spans, done):
                edges[rows, :] = new
            sums[...] = total
            return carry

        lax.fori_loop(0, edges.shape[0] // (ROWS * GROUP), step, 0)
        return sums[...]

    def node_step(current, summed, k):
        c_nin[k].wait()
        c_nout[k].wait()
        joined = jnp.concatenate([current, summed.astype(BF16)], axis=1)
        hidden = silu(dot(joined, nin[k])).astype(BF16)
        normed = layer_norm(dot(hidden, nout[k]), gain_ref[k, 1:2, :], bias_ref[k, 1:2, :])
        return current.astype(F32) + normed

    c_w0.wait()
    c_g2m.wait()

    def enc_first(rows):
        joined = jnp.concatenate([edge_v[rows, :], onehot(idx_a[rows, :], cells, cells)], axis=1)
        pre[rows, :] = dot(joined, tab[0:width + cells, :])

    over_rows(edge_v.shape[0], enc_first)
    c_recv0.wait()
    tab[recv_at:recv_at + node_count, :] = dot(mesh_ref[...], wproj[0, 1]).astype(BF16)
    c_eout[0].wait()

    mark_receivers(g2m_r_ref, inc_g)

    even = lat % 2 == 0
    up, down = lat > 0, lat < n_lat - 1
    near = jnp.where(even, 2 * cells, 0)
    far = 2 * cells - near

    def tile_part(spot_base):
        start = jnp.where(spot_base == 0, north_at, south_at)
        return tab[pl.ds(pl.multiple_of(start, cells), cells), :]

    for c in to_level:
        c.wait()

    @pl.when(up)
    def _():
        for c in to_south[1:]:
            c.wait_recv()

    @pl.when(down)
    def _():
        for c in to_north[1:]:
            c.wait_recv()

    @pl.when(jnp.logical_and(even, down))
    def _():
        to_north[0].wait_recv()

    @pl.when(jnp.logical_not(even))
    def _():
        to_south[0].wait_recv()

    def enc_near(rows):
        spots = idx_a[rows, :]
        rest = jnp.concatenate(
            [onehot(spots, 3 * cells, LANES), onehot(idx_b[rows, :], 0, node_count)], axis=1
        )
        acc = pre[rows, :] + dot(rest, tab[side_at:recv_at + node_count, :])
        pre[rows, :] = acc + dot(onehot(spots, near, cells), tile_part(near))

    over_rows(edge_v.shape[0], enc_near)

    @pl.when(jnp.logical_and(even, up))
    def _():
        to_south[0].wait_recv()

    @pl.when(jnp.logical_and(jnp.logical_not(even), down))
    def _():
        to_north[0].wait_recv()

    def enc_far(rows):
        return pre[rows, :] + dot(onehot(idx_a[rows, :], far, cells), tile_part(far))

    summed = finish_edges(enc_far, edge_v, inc_g, 0)
    nodes[...] = node_step(mesh_ref[...], summed, 0).astype(BF16)

    @pl.when(up)
    def _():
        for c in to_north:
            c.wait_send()

    @pl.when(down)
    def _():
        for c in to_south:
            c.wait_send()

    stride = next(i for i in range(n_dev // 3 + 1, 2 * n_dev) if math.gcd(i, n_dev) == 1)
    r_at, s_at, arr_at = width, width + node_count, width + 2 * node_count
    for k in range(1, blocks):
        table, pick = stk.at[k - 1], picks.at[k - 1]
        current = nodes[...]
        c_ps[k].wait()
        outgoing = dot(current, wproj[k, 0]).astype(BF16)
        pick[...] = dot(sel_send[...], outgoing).astype(BF16)

        def exchange(d, src_at, sem_at, to):
            return pltpu.make_async_remote_copy(
                src_ref=pick.at[pl.ds(pl.multiple_of(d * cap, cap), cap)],
                dst_ref=table.at[pl.ds(pl.multiple_of(arr_at + src_at * cap, cap), cap)],
                send_sem=a2a_send.at[k - 1, d], recv_sem=a2a_recv.at[k - 1, sem_at],
                device_id=place(to), device_id_type=MESH_IDS,
            )

        def send(off, carry):
            d = (me + off * stride) % n_dev
            exchange(d, me, me, d).start()
            return carry

        lax.fori_loop(1, n_dev, send, 0)
        table[pl.ds(pl.multiple_of(arr_at + me * cap, cap), cap), :] = pick[
            pl.ds(pl.multiple_of(me * cap, cap), cap), :
        ]
        table[s_at:s_at + node_count, :] = outgoing
        c_pr[k].wait()
        table[r_at:r_at + node_count, :] = dot(current, wproj[k, 1]).astype(BF16)
        c_w[k].wait()
        if k == 1:
            c_mm.wait()

        def mm_first(rows):
            joined = jnp.concatenate(
                [
                    mme_v[rows, :],
                    onehot(idx_d[rows, :], 0, node_count),
                    onehot(idx_c[rows, :], 0, node_count),
                ],
                axis=1,
            )
            pre[rows, :] = dot(joined, table[0:arr_at, :])

        over_rows(mme_v.shape[0], mm_first)
        if k == 1:
            mark_receivers(mm_r_ref, inc_m)

            def mark_arrived(rows):
                sel_arr[rows, :] = onehot(idx_c[rows, :], node_count, n_dev * cap)

            over_rows(mme_v.shape[0], mark_arrived)
        c_eout[k].wait()

        def arrive(off, carry):
            d = (me + off * stride) % n_dev
            exchange(d, d, d, d).wait()
            return carry

        lax.fori_loop(1, n_dev, arrive, 0)

        def mm_second(rows):
            return pre[rows, :] + dot(sel_arr[rows, :], table[arr_at:arr_at + n_dev * cap, :])

        summed = finish_edges(mm_second, mme_v, inc_m, k)
        updated = node_step(current, summed, k)
        if k < blocks - 1:
            nodes[...] = updated.astype(BF16)
        else:
            out_ref[...] = updated


def local(
    n_lat, n_lon,
    grid_latent, mesh_latent, g2m_edges, g2m_senders, g2m_receivers, mm_edges, mm_senders,
    mm_receivers, send_rows, edge_in, edge_out, node_in, node_out, norm_gain, norm_bias,
):
    tile_rows, tile_cols, width = grid_latent.shape
    blocks = edge_in.shape[0]
    node_count = mesh_latent.shape[0]
    n_dev = n_lat * n_lon
    edges, mm = g2m_edges.shape[0], mm_edges.shape[0]
    sends = send_rows.shape[1]
    assert tile_rows == HALO and node_count == LANES and tile_cols % LANES == 0
    node_in = node_in.reshape(blocks, 2 * width, width)
    hbm, vmem = pl.BlockSpec(memory_space=pl.ANY), pl.BlockSpec(memory_space=pltpu.VMEM)
    table_rows = width + 3 * tile_rows * tile_cols + LANES + node_count
    dma = pltpu.SemaphoreType.DMA
    done = pl.pallas_call(
        functools.partial(kernel, n_lat, n_lon, tile_rows, tile_cols, blocks),
        out_shape=jax.ShapeDtypeStruct((node_count, width), F32),
        in_specs=[hbm] * 15,
        out_specs=vmem,
        scratch_shapes=[
            pltpu.VMEM(mesh_latent.shape, BF16),
            pltpu.VMEM((1, edges), jnp.int32),
            pltpu.VMEM((1, edges), jnp.int32),
            pltpu.VMEM((1, mm), jnp.int32),
            pltpu.VMEM((1, mm), jnp.int32),
            pltpu.VMEM((1, sends), jnp.int32),
            pltpu.VMEM(norm_gain.shape, F32),
            pltpu.VMEM(norm_bias.shape, F32),
            pltpu.VMEM((mm, sends), BF16),
            pltpu.VMEM((node_count, edges), BF16),
            pltpu.VMEM((node_count, mm), BF16),
            pltpu.VMEM((node_count, width), F32),
            pltpu.VMEM((tile_rows, tile_cols, width), BF16),
            pltpu.VMEM((edges, width), BF16),
            pltpu.VMEM((mm, width), BF16),
            pltpu.VMEM((max(edges, mm), width), F32),
            pltpu.VMEM((table_rows, width), BF16),
            pltpu.VMEM((blocks - 1, width + 2 * node_count + sends, width), BF16),
            pltpu.VMEM((blocks, 2, width, width), BF16),
            pltpu.VMEM((blocks, width, width), BF16),
            pltpu.VMEM((blocks, 2 * width, width), BF16),
            pltpu.VMEM((blocks, width, width), BF16),
            pltpu.VMEM((2 * tile_rows * HALO, width), BF16),
            pltpu.VMEM((blocks - 1, sends, width), BF16),
            pltpu.VMEM((sends, node_count), BF16),
            pltpu.VMEM((edges, LANES), jnp.int32),
            pltpu.VMEM((edges, LANES), jnp.int32),
            pltpu.VMEM((mm, LANES), jnp.int32),
            pltpu.VMEM((mm, LANES), jnp.int32),
            pltpu.VMEM((node_count, width), BF16),
            dma((14 + 6 * blocks,)),
            dma((8,)),
            dma((8,)),
            dma((blocks - 1, n_dev)),
            dma((blocks - 1, n_dev)),
        ],
        compiler_params=pltpu.CompilerParams(
            collective_id=0, has_side_effects=True, vmem_limit_bytes=56 * 1024 * 1024
        ),
        name="encode_process",
    )(
        grid_latent, mesh_latent, g2m_edges, g2m_senders, g2m_receivers, mm_edges, mm_senders,
        mm_receivers, send_rows, edge_in, edge_out, node_in, node_out, norm_gain, norm_bias,
    )
    return done.astype(BF16)


def solution(mesh):
    tiles = P(("lat", "lon"), None)
    in_specs = (P("lat", "lon", None),) + (tiles,) * 8 + (P(),) * 6
    body = functools.partial(local, mesh.shape["lat"], mesh.shape["lon"])
    return jax.shard_map(body, mesh=mesh, in_specs=in_specs, out_specs=tiles, check_vma=False)
```

```python
import functools

import jax
import jax.numpy as jnp
from jax import lax
from jax.experimental import pallas as pl
from jax.experimental.pallas import tpu as pltpu
from jax.sharding import PartitionSpec as P

HALO = 4
NORM_EPS = 1e-05
LANES = 128
ROWS = 256
GROUP = 2
MESH_IDS = pl.DeviceIdType.MESH
BF16 = jnp.bfloat16
F32 = jnp.float32


def dot(a, b):
    return jnp.dot(a, b, preferred_element_type=F32)


def silu(v):
    half = 0.5 * v
    return half + half * jnp.tanh(half)


def layer_norm(values, gain, bias):
    scale = 1.0 / values.shape[-1]
    centre = jnp.sum(values, axis=-1, keepdims=True) * scale
    away = values - centre
    spread = jnp.sum(away * away, axis=-1, keepdims=True) * scale
    return away * lax.rsqrt(spread + NORM_EPS) * gain + bias


def onehot(idx, base, width):
    lane = lax.broadcasted_iota(jnp.int32, idx.shape, 1)
    parts = [
        jnp.where(idx == lane + (base + j), 1.0, 0.0).astype(BF16)
        for j in range(0, width, LANES)
    ]
    return parts[0] if len(parts) == 1 else jnp.concatenate(parts, axis=1)


def kernel(
    n_lat, n_lon, tile_rows, tile_cols, blocks,
    grid_hbm, mesh_hbm, g2m_hbm, g2m_s_hbm, g2m_r_hbm, mm_hbm, mm_s_hbm, mm_r_hbm, send_hbm,
    ein_hbm, eout_hbm, nin_hbm, nout_hbm, gain_hbm, bias_hbm,
    out_ref,
    mesh_ref, g2m_s_ref, g2m_r_ref, mm_s_ref, mm_r_ref, send_ref, gain_ref, bias_ref,
    sel_arr, inc_g, inc_m, sums, node_pre, grid_v, edge_v, mme_v, pre, tab, stk, wproj, eout, nin, nout,
    packs, picks, sel_send, idx_a, idx_b, idx_c, idx_d, nodes,
    w_sem, halo_send, halo_recv, a2a_send, a2a_recv,
):
    lat, lon = lax.axis_index("lat"), lax.axis_index("lon")
    n_dev = n_lat * n_lon
    me = lat * n_lon + lon
    width = mesh_ref.shape[1]
    node_count = mesh_ref.shape[0]
    cells = tile_rows * tile_cols
    cap = send_ref.shape[1] // n_dev
    barrier = pltpu.get_barrier_semaphore()

    def place(d):
        return (d // n_lon, d % n_lon)

    def greet(off, carry):
        d = (me + off) % n_dev
        pl.semaphore_signal(barrier, inc=1, device_id=place(d), device_id_type=MESH_IDS)
        return carry


    def load(src, dst, at):
        copy = pltpu.make_async_copy(src, dst, w_sem.at[at])
        copy.start()
        return copy

    own_at, north_at, south_at = width, width + cells, width + 2 * cells
    side_at = width + 3 * cells
    recv_at = side_at + LANES

    c_grid = load(grid_hbm, grid_v, 0)
    c_proj0 = load(ein_hbm.at[0, 1], wproj.at[0, 0], 1)
    c_w0 = load(ein_hbm.at[0, 0], tab.at[pl.ds(0, width)], 2)
    c_g2m = load(g2m_hbm, edge_v, 3)
    c_recv0 = load(ein_hbm.at[0, 2], wproj.at[0, 1], 4)
    small = [
        load(src, dst, 5 + i)
        for i, (src, dst) in enumerate((
            (g2m_s_hbm, g2m_s_ref), (g2m_r_hbm, g2m_r_ref), (mm_s_hbm, mm_s_ref),
            (mm_r_hbm, mm_r_ref), (send_hbm, send_ref), (mesh_hbm, mesh_ref),
            (gain_hbm, gain_ref), (bias_hbm, bias_ref),
        ))
    ]
    lax.fori_loop(1, n_dev, greet, 0)

    tall = tile_rows + 2 * HALO
    wide = tile_cols + 2 * HALO
    zero_rows = functools.partial(jnp.zeros, dtype=BF16)
    side_rows = 2 * tall * HALO
    tab[side_at + side_rows:recv_at, :] = zero_rows((LANES - side_rows, width))
    block = tile_rows * HALO

    @pl.when(lat == 0)
    def _():
        tab[north_at:north_at + cells, :] = zero_rows((cells, width))
        tab[side_at:side_at + block, :] = zero_rows((block, width))
        tab[side_at + 3 * block:side_at + 4 * block, :] = zero_rows((block, width))

    @pl.when(lat == n_lat - 1)
    def _():
        tab[south_at:south_at + cells, :] = zero_rows((cells, width))
        tab[side_at + 2 * block:side_at + 3 * block, :] = zero_rows((block, width))
        tab[side_at + 5 * block:side_at + 6 * block, :] = zero_rows((block, width))

    c_grid.wait()
    c_proj0.wait()
    firsts, lasts = [], []
    for r in range(tile_rows):
        term = dot(grid_v[r], wproj[0, 0])
        tab[own_at + r * tile_cols:own_at + (r + 1) * tile_cols, :] = term.astype(BF16)
        firsts.append(term[:HALO])
        lasts.append(term[tile_cols - HALO:])
    packs[0:block, :] = jnp.concatenate(firsts, axis=0).astype(BF16)
    packs[block:2 * block, :] = jnp.concatenate(lasts, axis=0).astype(BF16)

    pl.semaphore_wait(barrier, n_dev - 1)

    own = tab.at[pl.ds(own_at, cells)]
    east, west = (lon + 1) % n_lon, (lon + n_lon - 1) % n_lon

    def halo(at, src, dst_row, count, to):
        return pltpu.make_async_remote_copy(
            src_ref=src, dst_ref=tab.at[pl.ds(dst_row, count)],
            send_sem=halo_send.at[at], recv_sem=halo_recv.at[at],
            device_id=to, device_id_type=MESH_IDS,
        )

    first_cols, last_cols = packs.at[pl.ds(0, block)], packs.at[pl.ds(block, block)]
    to_north = [
        halo(0, own, south_at, cells, (lat - 1, lon)),
        halo(1, last_cols, side_at + 2 * block, block, (lat - 1, east)),
        halo(2, first_cols, side_at + 5 * block, block, (lat - 1, west)),
    ]
    to_south = [
        halo(3, own, north_at, cells, (lat + 1, lon)),
        halo(4, last_cols, side_at, block, (lat + 1, east)),
        halo(5, first_cols, side_at + 3 * block, block, (lat + 1, west)),
    ]
    to_level = [
        halo(6, last_cols, side_at + block, block, (lat, east)),
        halo(7, first_cols, side_at + 4 * block, block, (lat, west)),
    ]

    for c in to_level:
        c.start()

    @pl.when(lat > 0)
    def _():
        for c in reversed(to_north):
            c.start()

    @pl.when(lat < n_lat - 1)
    def _():
        for c in reversed(to_south):
            c.start()

    c_eout, c_nin, c_nout, c_w, c_ps, c_pr = [], [], [], [None], [None], [None]
    at = 5 + len(small)
    for k in range(blocks):
        if k == 1:
            c_mm = load(mm_hbm, mme_v, at)
            at += 1
        if k > 0:
            c_ps.append(load(ein_hbm.at[k, 1], wproj.at[k, 0], at))
            c_pr.append(load(ein_hbm.at[k, 2], wproj.at[k, 1], at + 1))
            c_w.append(load(ein_hbm.at[k, 0], stk.at[k - 1, pl.ds(0, width)], at + 2))
            at += 3
        c_eout.append(load(eout_hbm.at[k], eout.at[k], at))
        c_nin.append(load(nin_hbm.at[k], nin.at[k], at + 1))
        c_nout.append(load(nout_hbm.at[k], nout.at[k], at + 2))
        at += 3

    for c in small:
        c.wait()

    senders = g2m_s_ref[...]
    row = jnp.zeros_like(senders)
    for r in range(1, tall):
        row = row + jnp.where(senders >= r * wide, 1, 0)
    col = senders - row * wide
    west_spot = 3 * cells + row * HALO + col
    east_spot = 3 * cells + (tall + row) * HALO + (col - (wide - HALO))
    spot = jnp.where(
        col < HALO, west_spot,
        jnp.where(col >= wide - HALO, east_spot, row * tile_cols + col - HALO),
    )

    def spread_rows(values, dst):
        for j in range(0, values.shape[1], LANES):
            piece = jnp.broadcast_to(values[:, j:j + LANES], (LANES, LANES))
            dst[j:j + LANES, :] = piece.T

    spread_rows(spot, idx_a)
    spread_rows(g2m_r_ref[...], idx_b)
    spread_rows(mm_s_ref[...], idx_c)
    spread_rows(jnp.minimum(mm_r_ref[...], node_count - 1), idx_d)
    sends = send_ref[...]
    for j in range(0, sends.shape[1], LANES):
        piece = jnp.broadcast_to(sends[:, j:j + LANES], (LANES, LANES)).T
        sel_send[j:j + LANES, :] = onehot(piece, 0, node_count)

    def over_rows(count, body):
        def step(i, carry):
            for g in range(GROUP):
                body(pl.ds(pl.multiple_of((i * GROUP + g) * ROWS, ROWS), ROWS))
            return carry

        lax.fori_loop(0, count // (ROWS * GROUP), step, 0)

    def mark_receivers(recv_ref, dst):
        node = lax.broadcasted_iota(jnp.int32, dst.shape, 0)
        dst[...] = jnp.where(node == recv_ref[...], 1.0, 0.0).astype(BF16)

    def finish_edges(first, edges, incidence, k):
        sums[...] = jnp.zeros_like(sums)
        gain, bias = gain_ref[k, 0:1, :], bias_ref[k, 0:1, :]

        def step(i, carry):
            spans = [
                pl.ds(pl.multiple_of((i * GROUP + g) * ROWS, ROWS), ROWS) for g in range(GROUP)
            ]
            total = sums[...]
            done = []
            ahead = first(spans[0])
            for g, rows in enumerate(spans):
                acc = ahead
                if g + 1 < GROUP:
                    ahead = first(spans[g + 1])
                hidden = silu(acc).astype(BF16)
                normed = layer_norm(dot(hidden, eout[k]), gain, bias)
                new = (edges[rows, :].astype(F32) + normed).astype(BF16)
                total = total + dot(incidence[:, rows], new)
                done.append(new)
            for rows, new in zip(spans, done):
                edges[rows, :] = new
            sums[...] = total
            return carry

        lax.fori_loop(0, edges.shape[0] // (ROWS * GROUP), step, 0)
        return sums[...]

    def node_first(current, k):
        c_nin[k].wait()
        c_nout[k].wait()
        node_pre[...] = dot(current, nin[k, 0:width, :])

    def node_step(current, summed, k):
        acc = node_pre[...] + dot(summed.astype(BF16), nin[k, width:2 * width, :])
        hidden = silu(acc).astype(BF16)
        normed = layer_norm(dot(hidden, nout[k]), gain_ref[k, 1:2, :], bias_ref[k, 1:2, :])
        return current.astype(F32) + normed

    c_w0.wait()
    c_g2m.wait()

    def enc_first(rows):
        joined = jnp.concatenate([edge_v[rows, :], onehot(idx_a[rows, :], cells, cells)], axis=1)
        pre[rows, :] = dot(joined, tab[0:width + cells, :])

    over_rows(edge_v.shape[0], enc_first)
    c_recv0.wait()
    tab[recv_at:recv_at + node_count, :] = dot(mesh_ref[...], wproj[0, 1]).astype(BF16)
    c_eout[0].wait()

    mark_receivers(g2m_r_ref, inc_g)
    node_first(mesh_ref[...], 0)

    even = lat % 2 == 0
    up, down = lat > 0, lat < n_lat - 1
    near = jnp.where(even, 2 * cells, 0)
    far = 2 * cells - near

    def tile_part(spot_base):
        start = jnp.where(spot_base == 0, north_at, south_at)
        return tab[pl.ds(pl.multiple_of(start, cells), cells), :]

    for c in to_level:
        c.wait()

    @pl.when(up)
    def _():
        for c in to_south[1:]:
            c.wait_recv()

    @pl.when(down)
    def _():
        for c in to_north[1:]:
            c.wait_recv()

    @pl.when(jnp.logical_and(even, down))
    def _():
        to_north[0].wait_recv()

    @pl.when(jnp.logical_not(even))
    def _():
        to_south[0].wait_recv()

    def enc_near(rows):
        spots = idx_a[rows, :]
        rest = jnp.concatenate(
            [onehot(spots, 3 * cells, LANES), onehot(idx_b[rows, :], 0, node_count)], axis=1
        )
        acc = pre[rows, :] + dot(rest, tab[side_at:recv_at + node_count, :])
        pre[rows, :] = acc + dot(onehot(spots, near, cells), tile_part(near))

    over_rows(edge_v.shape[0], enc_near)

    @pl.when(jnp.logical_and(even, up))
    def _():
        to_south[0].wait_recv()

    @pl.when(jnp.logical_and(jnp.logical_not(even), down))
    def _():
        to_north[0].wait_recv()

    def enc_far(rows):
        return pre[rows, :] + dot(onehot(idx_a[rows, :], far, cells), tile_part(far))

    summed = finish_edges(enc_far, edge_v, inc_g, 0)
    nodes[...] = node_step(mesh_ref[...], summed, 0).astype(BF16)

    @pl.when(up)
    def _():
        for c in to_north:
            c.wait_send()

    @pl.when(down)
    def _():
        for c in to_south:
            c.wait_send()

    pending = []
    r_at, s_at, arr_at = width, width + node_count, width + 2 * node_count
    for k in range(1, blocks):
        table, pick = stk.at[k - 1], picks.at[k - 1]
        current = nodes[...]
        c_ps[k].wait()
        outgoing = dot(current, wproj[k, 0]).astype(BF16)
        pick[...] = dot(sel_send[...], outgoing).astype(BF16)

        def exchange(d):
            return pltpu.make_async_remote_copy(
                src_ref=pick.at[pl.ds(pl.multiple_of(d * cap, cap), cap)],
                dst_ref=table.at[pl.ds(pl.multiple_of(arr_at + me * cap, cap), cap)],
                send_sem=a2a_send.at[k - 1], recv_sem=a2a_recv.at[k - 1],
                device_id=place(d), device_id_type=MESH_IDS,
            )

        def send(off, carry):
            d = (me + off) % n_dev
            exchange(d).start()
            return carry

        lax.fori_loop(1, n_dev, send, 0)
        table[pl.ds(pl.multiple_of(arr_at + me * cap, cap), cap), :] = pick[
            pl.ds(pl.multiple_of(me * cap, cap), cap), :
        ]
        table[s_at:s_at + node_count, :] = outgoing
        c_pr[k].wait()
        table[r_at:r_at + node_count, :] = dot(current, wproj[k, 1]).astype(BF16)
        c_w[k].wait()
        if k == 1:
            c_mm.wait()

        def mm_first(rows):
            joined = jnp.concatenate(
                [
                    mme_v[rows, :],
                    onehot(idx_d[rows, :], 0, node_count),
                    onehot(idx_c[rows, :], 0, node_count),
                ],
                axis=1,
            )
            pre[rows, :] = dot(joined, table[0:arr_at, :])

        over_rows(mme_v.shape[0], mm_first)
        if k == 1:
            mark_receivers(mm_r_ref, inc_m)

            def mark_arrived(rows):
                sel_arr[rows, :] = onehot(idx_c[rows, :], node_count, n_dev * cap)

            over_rows(mme_v.shape[0], mark_arrived)
        c_eout[k].wait()
        node_first(current, k)

        whole = pltpu.make_async_remote_copy(
            src_ref=pick.at[pl.ds(0, (n_dev - 1) * cap)],
            dst_ref=table.at[pl.ds(arr_at, (n_dev - 1) * cap)],
            send_sem=a2a_send.at[k - 1], recv_sem=a2a_recv.at[k - 1],
            device_id=place((me + 1) % n_dev), device_id_type=MESH_IDS,
        )
        whole.wait_recv()
        pending.append(whole)

        def mm_second(rows):
            return pre[rows, :] + dot(sel_arr[rows, :], table[arr_at:arr_at + n_dev * cap, :])

        summed = finish_edges(mm_second, mme_v, inc_m, k)
        updated = node_step(current, summed, k)
        if k < blocks - 1:
            nodes[...] = updated.astype(BF16)
        else:
            out_ref[...] = updated
    for whole in pending:
        whole.wait_send()


def local(
    n_lat, n_lon,
    grid_latent, mesh_latent, g2m_edges, g2m_senders, g2m_receivers, mm_edges, mm_senders,
    mm_receivers, send_rows, edge_in, edge_out, node_in, node_out, norm_gain, norm_bias,
):
    tile_rows, tile_cols, width = grid_latent.shape
    blocks = edge_in.shape[0]
    node_count = mesh_latent.shape[0]
    n_dev = n_lat * n_lon
    edges, mm = g2m_edges.shape[0], mm_edges.shape[0]
    sends = send_rows.shape[1]
    assert tile_rows == HALO and node_count == LANES and tile_cols % LANES == 0
    node_in = node_in.reshape(blocks, 2 * width, width)
    hbm, vmem = pl.BlockSpec(memory_space=pl.ANY), pl.BlockSpec(memory_space=pltpu.VMEM)
    table_rows = width + 3 * tile_rows * tile_cols + LANES + node_count
    dma = pltpu.SemaphoreType.DMA
    done = pl.pallas_call(
        functools.partial(kernel, n_lat, n_lon, tile_rows, tile_cols, blocks),
        out_shape=pltpu.VMEM((node_count, width), F32),
        in_specs=[hbm] * 15,
        out_specs=vmem,
        scratch_shapes=[
            pltpu.VMEM(mesh_latent.shape, BF16),
            pltpu.VMEM((1, edges), jnp.int32),
            pltpu.VMEM((1, edges), jnp.int32),
            pltpu.VMEM((1, mm), jnp.int32),
            pltpu.VMEM((1, mm), jnp.int32),
            pltpu.VMEM((1, sends), jnp.int32),
            pltpu.VMEM(norm_gain.shape, F32),
            pltpu.VMEM(norm_bias.shape, F32),
            pltpu.VMEM((mm, sends), BF16),
            pltpu.VMEM((node_count, edges), BF16),
            pltpu.VMEM((node_count, mm), BF16),
            pltpu.VMEM((node_count, width), F32),
            pltpu.VMEM((node_count, width), F32),
            pltpu.VMEM((tile_rows, tile_cols, width), BF16),
            pltpu.VMEM((edges, width), BF16),
            pltpu.VMEM((mm, width), BF16),
            pltpu.VMEM((max(edges, mm), width), F32),
            pltpu.VMEM((table_rows, width), BF16),
            pltpu.VMEM((blocks - 1, width + 2 * node_count + sends, width), BF16),
            pltpu.VMEM((blocks, 2, width, width), BF16),
            pltpu.VMEM((blocks, width, width), BF16),
            pltpu.VMEM((blocks, 2 * width, width), BF16),
            pltpu.VMEM((blocks, width, width), BF16),
            pltpu.VMEM((2 * tile_rows * HALO, width), BF16),
            pltpu.VMEM((blocks - 1, sends, width), BF16),
            pltpu.VMEM((sends, node_count), BF16),
            pltpu.VMEM((edges, LANES), jnp.int32),
            pltpu.VMEM((edges, LANES), jnp.int32),
            pltpu.VMEM((mm, LANES), jnp.int32),
            pltpu.VMEM((mm, LANES), jnp.int32),
            pltpu.VMEM((node_count, width), BF16),
            dma((14 + 6 * blocks,)),
            dma((8,)),
            dma((8,)),
            dma((blocks - 1,)),
            dma((blocks - 1,)),
        ],
        compiler_params=pltpu.CompilerParams(
            collective_id=0, has_side_effects=True, vmem_limit_bytes=56 * 1024 * 1024
        ),
        name="encode_process",
    )(
        grid_latent, mesh_latent, g2m_edges, g2m_senders, g2m_receivers, mm_edges, mm_senders,
        mm_receivers, send_rows, edge_in, edge_out, node_in, node_out, norm_gain, norm_bias,
    )
    return done.astype(BF16)


def solution(mesh):
    tiles = P(("lat", "lon"), None)
    in_specs = (P("lat", "lon", None),) + (tiles,) * 8 + (P(),) * 6
    body = functools.partial(local, mesh.shape["lat"], mesh.shape["lon"])
    return jax.shard_map(body, mesh=mesh, in_specs=in_specs, out_specs=tiles, check_vma=False)
```
